512 devices in a mesh: sta: 64 (over z_lo, x, core), win: 8 (over y, z_hi).
Axes of the slice: x: 4, y: 4, z: 16 (z_hi: 2, z_lo: 8; z = z_hi * 8 + z_lo), core: 2. Of those that a mesh axis runs over, the one named last changes fastest.
Arguments:
- spectra: bfloat16 [2, 8, 256, 2048], P(None, 'win', 'sta'), may hold values from -500 to 500
- quality: int32 [8, 256], P('win', 'sta'), may hold values 0 or 1
- block_mask: int32 [64, 64], P('sta'), may hold values 0 or 1
Outputs:
- correlations: bfloat16 [256, 256, 256], P('sta', 'win')
The draws below stay inside these ranges and needn't reach their ends.
All inputs are finite; a program needn't handle non-finite values. No bound on the sum of `quality` or of `block_mask` on one device may be relied on, other than what follows from the above.
Results may differ from the reference program's by a relative error of at most 0.0066.
Values may be sent and summed in bfloat16 or wider, within the bound.
No kernel may reach another device: no remote copies, remote signals or barrier semaphores. Data moves between devices by JAX's collectives and lax.ppermute only.
A program may use at most 64 MiB of HBM per device.

```python
import math
import jax
import jax.numpy as jnp
from jax import lax

SB = 4
WD = 1
F = 2048
LAGS = 256
STATIONS = 256
WINDOWS = 8
N_STA = 64
N_WIN = 8


def draw_spectra(key, part):
    key_base, key_row, key_bin = jax.random.split(key, 3)
    full_shape = (2, WINDOWS, STATIONS, F)
    row_scale = jnp.exp(jax.random.uniform(key_row, (1, WINDOWS, STATIONS, 1), jnp.float32) * jnp.log(10.0))
    bin_scale = jnp.exp(jax.random.uniform(key_bin, (1, 1, 1, F), jnp.float32) * jnp.log(10.0))
    base_values = jax.random.normal(key_base, full_shape, jnp.float32)
    base_values = jnp.clip(base_values, -5.0, 5.0)
    return (base_values * row_scale * bin_scale).astype(jnp.bfloat16)


def set_ends(values, own_key, low, high):
    longest = values.shape.index(max(values.shape))
    spots = []
    for shift in (0, 1):
        where = [jax.random.randint(jax.random.fold_in(own_key, axis), (), 0, length) for axis, length in enumerate(values.shape)]
        where[longest] = (where[longest] + shift) % values.shape[longest]
        spots.append(tuple(where))
    return values.at[spots[0]].set(low).at[spots[1]].set(high)


def setup_inputs(seed: int = 0) -> dict:
    key_of = jax.random.split(jax.random.key(seed), 4)
    spectra = draw_spectra(jax.random.fold_in(key_of[3], 71), 0)
    quality = set_ends((jax.random.randint(key_of[1], (WINDOWS, STATIONS), 0, 4) < 3).astype(jnp.int32), jax.random.fold_in(key_of[1], 1), 0, 1)
    block_mask = set_ends((jax.random.randint(key_of[2], (N_STA, N_STA), 0, 4) < 3).astype(jnp.int32), jax.random.fold_in(key_of[2], 1), 0, 1)
    return dict(spectra=spectra, quality=quality, block_mask=block_mask)


def whiten(spectra, quality):
    values = spectra.astype(jnp.float32)
    power_mean = lax.optimization_barrier(jnp.mean(values[0] * values[0] + values[1] * values[1], axis=-1, keepdims=True))
    flags = quality.astype(jnp.float32)[:, :, None]
    return (values * (lax.rsqrt(power_mean + 1e-06) * flags)[None]).astype(jnp.bfloat16)

def lag_table(bins_count, lag_count):
    freq_index = jnp.arange(bins_count, dtype=jnp.int32)[:, None]
    lag_index = jnp.arange(lag_count, dtype=jnp.int32)[None, :] - lag_count // 2
    phase = freq_index * lag_index % (2 * bins_count)
    angles = phase.astype(jnp.float32) * jnp.float32(math.pi / bins_count)
    norm_scale = jnp.float32(1.0 / math.sqrt(bins_count))
    stacked = jnp.concatenate([jnp.cos(angles), -jnp.sin(angles)], axis=0) * norm_scale
    return stacked.astype(jnp.bfloat16)

def reference(spectra, quality, block_mask):
    white = whiten(spectra, quality).astype(jnp.float32)
    white_groups = white.reshape(2, N_WIN, WD, STATIONS, F)
    basis_table = lag_table(F, LAGS).astype(jnp.float32)

    def one_block(block_id):
        own_part = lax.dynamic_slice_in_dim(white_groups, block_id * SB, SB, axis=3)
        real_part = jnp.einsum('gwif,gwjf->gijf', own_part[0], white_groups[0]) + jnp.einsum('gwif,gwjf->gijf', own_part[1], white_groups[1])
        imag_part = jnp.einsum('gwif,gwjf->gijf', own_part[1], white_groups[0]) - jnp.einsum('gwif,gwjf->gijf', own_part[0], white_groups[1])
        cross_rounded = jnp.concatenate([real_part, imag_part], axis=-1).astype(jnp.bfloat16)
        cross_rounded = lax.optimization_barrier(cross_rounded)
        cross_values = cross_rounded.astype(jnp.float32)
        partial_sums = jnp.dot(cross_values.reshape(-1, 2 * F), basis_table, preferred_element_type=jnp.float32, precision=lax.Precision.HIGHEST)
        total = lax.optimization_barrier(jnp.sum(partial_sums.reshape(N_WIN, SB, STATIONS, LAGS), axis=0))
        pair_mask = jnp.repeat(block_mask[block_id].astype(jnp.float32), SB)
        return (total * pair_mask[None, :, None]).astype(jnp.bfloat16)
    blocks = lax.map(one_block, jnp.arange(N_STA, dtype=jnp.int32))
    return blocks.reshape(STATIONS, STATIONS, LAGS)
```

```python
import functools
import math

import jax
import jax.numpy as jnp
import ml_dtypes
import numpy as np
from jax import lax
from jax.experimental import pallas as pl
from jax.experimental.pallas import tpu as pltpu
from jax.sharding import Mesh, PartitionSpec as P

LAGS = 256
BINS = 2048
CHUNK = 256
GRID = (("zl", 8), ("x", 4), ("core", 2), ("y", 4), ("zh", 2))
STA = ("zl", "x", "core")
WIN = ("y", "zh")


def lag_table():
    phase = np.arange(BINS)[:, None] * (np.arange(LAGS)[None, :] - LAGS // 2) % (2 * BINS)
    angles = phase.astype(np.float32) * np.float32(math.pi / BINS)
    scale = np.float32(1.0 / math.sqrt(BINS))
    both = np.concatenate([np.cos(angles), -np.sin(angles)], axis=0).astype(np.float32) * scale
    return both.astype(ml_dtypes.bfloat16)


def whiten(spectra, quality):
    values = spectra.astype(jnp.float32)
    power_mean = jnp.mean(values[0] * values[0] + values[1] * values[1], axis=-1, keepdims=True)
    flags = quality.astype(jnp.float32)[:, :, None]
    return (values * (lax.rsqrt(power_mean + 1e-06) * flags)[None]).astype(jnp.bfloat16)


def pair_kernel(half_ref, far_ref, own_ref, table_ref, out_ref, far_re, far_im, own, cross, total, order):
    second = half_ref[0] == 1
    for w in range(2):
        for k in range(4):
            both = far_ref[pl.ds((w * 8 + 2 * k) * 8, 16), :].astype(jnp.float32)
            block = jnp.where(second, both[8:16], both[0:8])
            far_re[w, 4 * k : 4 * k + 4, :] = block[0:4]
            far_im[w, 4 * k : 4 * k + 4, :] = block[4:8]
    own[...] = own_ref[...].astype(jnp.float32)
    total[...] = jnp.zeros_like(total)

    @pl.loop(0, BINS // CHUNK)
    def _(c):
        at = pl.multiple_of(c * CHUNK, CHUNK)
        bins = pl.ds(at, CHUNK)

        @pl.loop(0, 8)
        def _(block):
            first = pl.multiple_of(block * 16, 16)
            b_re = [far_re[w, :, bins] for w in range(2)]
            b_im = [far_im[w, :, bins] for w in range(2)]
            for i in range(4):
                re, im = None, None
                for w in range(2):
                    a_re = own[pl.ds(first + w * 8 + i, 1), bins]
                    a_im = own[pl.ds(first + w * 8 + 4 + i, 1), bins]
                    re_w = a_re * b_re[w] + a_im * b_im[w]
                    im_w = a_im * b_re[w] - a_re * b_im[w]
                    re = re_w if re is None else re + re_w
                    im = im_w if im is None else im + im_w
                rows = pl.ds(pl.multiple_of(block * 64 + i * 16, 16), 16)
                cross[rows, 0:CHUNK] = re.astype(jnp.bfloat16)
                cross[rows, CHUNK : 2 * CHUNK] = im.astype(jnp.bfloat16)

        total[...] += jnp.dot(
            cross[:, 0:CHUNK], table_ref[bins, :], preferred_element_type=jnp.float32
        ) + jnp.dot(
            cross[:, CHUNK : 2 * CHUNK],
            table_ref[pl.ds(pl.multiple_of(BINS + at, CHUNK), CHUNK), :],
            preferred_element_type=jnp.float32,
        )

    for block in range(8):
        for i in range(4):
            rows = total[block * 64 + i * 16 : block * 64 + i * 16 + 16, :]
            for k in range(4):
                to = (block * 4 + k) * 16 + i * 4
                order[to : to + 4, :] = rows[4 * k : 4 * k + 4]
    out_ref[...] = order[...].astype(jnp.bfloat16)


def pairs(half, far, own, table):
    vmem = pl.BlockSpec(memory_space=pltpu.VMEM)
    return pl.pallas_call(
        pair_kernel,
        out_shape=jax.ShapeDtypeStruct((512, LAGS), jnp.bfloat16),
        in_specs=[pl.BlockSpec(memory_space=pltpu.SMEM), vmem, vmem, vmem],
        out_specs=vmem,
        scratch_shapes=[
            pltpu.VMEM((2, 16, BINS), jnp.float32),
            pltpu.VMEM((2, 16, BINS), jnp.float32),
            pltpu.VMEM((128, BINS), jnp.float32),
            pltpu.VMEM((512, 2 * CHUNK), jnp.bfloat16),
            pltpu.VMEM((512, LAGS), jnp.float32),
            pltpu.VMEM((512, LAGS), jnp.float32),
        ],
        compiler_params=pltpu.CompilerParams(vmem_limit_bytes=32 * 1024 * 1024),
    )(half, far, own, table)


def shards(table, spectra, quality, block_mask):
    white = whiten(spectra, quality).reshape(8, BINS)
    column = lax.all_gather(white, ("zh", "zl"))
    zl = lax.axis_index("zl")
    mine = lax.dynamic_slice_in_dim(column.reshape(2, 8, 8, BINS), zl, 1, axis=1)
    plane = lax.all_gather(mine.reshape(16, BINS), ("x", "core"))
    half = lax.axis_index("zh").astype(jnp.int32).reshape(1)
    partial = pairs(half, column.reshape(128, BINS), plane.reshape(128, BINS), table)
    parts = lax.all_to_all(partial.reshape(32, 16, LAGS), ("x", "core", "y"), 0, 0, tiled=True)
    summed = jnp.sum(parts.astype(jnp.float32).reshape(8, 4, 4, 4, LAGS), axis=1)
    group = lax.axis_index(WIN)
    mask = lax.dynamic_slice_in_dim(block_mask[0], group * 8, 8).astype(jnp.float32)
    summed = summed * mask[:, None, None, None]
    return summed.transpose(1, 0, 2, 3).reshape(4, 32, LAGS).astype(jnp.bfloat16)


def solution(mesh):
    names, sizes = zip(*GRID)
    fine = Mesh(mesh.devices.reshape(sizes), names)
    placed = (P(None, WIN, STA, None), P(WIN, STA), P(STA, None))
    table = lag_table()

    def run(spectra, quality, block_mask):
        body = functools.partial(shards, jnp.asarray(table))
        return jax.shard_map(
            body, mesh=fine, in_specs=placed, out_specs=P(STA, WIN, None), check_vma=False
        )(spectra, quality, block_mask)

    return run
```

```python
import functools
import math

import jax
import jax.numpy as jnp
import ml_dtypes
import numpy as np
from jax import lax
from jax.experimental import pallas as pl
from jax.experimental.pallas import tpu as pltpu
from jax.sharding import Mesh, PartitionSpec as P

LAGS = 256
BINS = 2048
CHUNK = 256
CHUNKS = BINS // CHUNK
GRID = (("zl", 8), ("x", 4), ("core", 2), ("y", 4), ("zh", 2))
STA = ("zl", "x", "core")
WIN = ("y", "zh")
VMEM = pl.BlockSpec(memory_space=pltpu.VMEM)
SMEM = pl.BlockSpec(memory_space=pltpu.SMEM)


def lag_table():
    phase = np.arange(BINS)[:, None] * (np.arange(LAGS)[None, :] - LAGS // 2) % (2 * BINS)
    angles = phase.astype(np.float32) * np.float32(math.pi / BINS)
    scale = np.float32(1.0 / math.sqrt(BINS))
    both = np.stack([np.cos(angles), -np.sin(angles)]).astype(np.float32) * scale
    both = both.reshape(2, CHUNKS, CHUNK, LAGS).transpose(1, 0, 2, 3).reshape(2 * BINS, LAGS)
    return both.astype(ml_dtypes.bfloat16)


def whiten_kernel(quality_ref, spectra_ref, white_ref):
    re = spectra_ref[0, 0].astype(jnp.float32)
    im = spectra_ref[1, 0].astype(jnp.float32)
    power_mean = jnp.mean(re * re + im * im, axis=-1, keepdims=True)
    row = lax.broadcasted_iota(jnp.int32, (4, 1), 0)
    flags = jnp.zeros((4, 1), jnp.float32)
    for s in range(4):
        flags = jnp.where(row == s, quality_ref[0, s].astype(jnp.float32), flags)
    scale = lax.rsqrt(power_mean + 1e-06) * flags
    white_ref[...] = jnp.concatenate([re * scale, im * scale], axis=0).astype(jnp.bfloat16)


def whiten(spectra, quality):
    return pl.pallas_call(
        whiten_kernel,
        out_shape=jax.ShapeDtypeStruct((8, BINS), jnp.bfloat16),
        in_specs=[SMEM, VMEM],
        out_specs=VMEM,
    )(quality, spectra)


def pair_kernel(
    place_ref, mine_ref, other_ref, own_ref, table_hbm, out_ref,
    far_re, far_im, own, cross_even, cross_odd, total, order, table, arrived,
):
    fetch = pltpu.make_async_copy(table_hbm, table, arrived)
    fetch.start()
    second = place_ref[0] == 1
    core = place_ref[1]
    for column_ref, side in ((mine_ref, core), (other_ref, 1 - core)):
        for w in range(2):
            for k in range(4):
                both = column_ref[pl.ds((w * 8 + 2 * k) * 8, 16), :].astype(jnp.float32)
                block = jnp.where(second, both[8:16], both[0:8])
                far_re[side, w, 4 * k : 4 * k + 4, :] = block[0:4]
                far_im[side, w, 4 * k : 4 * k + 4, :] = block[4:8]
    own[...] = own_ref[...].astype(jnp.float32)
    total[...] = jnp.zeros_like(total)

    def products(c, cross):
        bins = pl.ds(pl.multiple_of(c * CHUNK, CHUNK), CHUNK)
        for side in range(2):
            b_re = [far_re[side, w, :, bins] for w in range(2)]
            b_im = [far_im[side, w, :, bins] for w in range(2)]
            for i in range(16):
                re, im = None, None
                for w in range(2):
                    at = (i // 4) * 16 + w * 8 + i % 4
                    a_re = own[at : at + 1, bins]
                    a_im = own[at + 4 : at + 5, bins]
                    re_w = a_re * b_re[w] + a_im * b_im[w]
                    im_w = a_im * b_re[w] - a_re * b_im[w]
                    re = re_w if re is None else re + re_w
                    im = im_w if im is None else im + im_w
                to = side * 256 + i * 16
                cross[to : to + 16, 0:CHUNK] = re.astype(jnp.bfloat16)
                cross[to : to + 16, CHUNK : 2 * CHUNK] = im.astype(jnp.bfloat16)

    def to_lags(c, cross):
        rows = pl.ds(pl.multiple_of(c * 2 * CHUNK, 2 * CHUNK), 2 * CHUNK)
        total[...] += jnp.dot(cross[...], table[rows, :], preferred_element_type=jnp.float32)

    products(0, cross_even)
    fetch.wait()

    @pl.loop(0, CHUNKS // 2 - 1)
    def _(c):
        products(2 * c + 1, cross_odd)
        to_lags(2 * c, cross_even)
        products(2 * c + 2, cross_even)
        to_lags(2 * c + 1, cross_odd)

    products(CHUNKS - 1, cross_odd)
    to_lags(CHUNKS - 2, cross_even)
    to_lags(CHUNKS - 1, cross_odd)

    for side in range(2):
        for i in range(16):
            rows = total[side * 256 + i * 16 : side * 256 + i * 16 + 16, :]
            for k in range(4):
                to = ((i // 4) * 4 + k) * 32 + (i % 4) * 8 + side * 4
                order[to : to + 4, :] = rows[4 * k : 4 * k + 4]
    out_ref[...] = order[...].astype(jnp.bfloat16)


def pairs(place, mine, other, own, table):
    return pl.pallas_call(
        pair_kernel,
        out_shape=jax.ShapeDtypeStruct((512, LAGS), jnp.bfloat16),
        in_specs=[SMEM, VMEM, VMEM, VMEM, pl.BlockSpec(memory_space=pl.ANY)],
        out_specs=VMEM,
        scratch_shapes=[
            pltpu.VMEM((2, 2, 16, BINS), jnp.float32),
            pltpu.VMEM((2, 2, 16, BINS), jnp.float32),
            pltpu.VMEM((64, BINS), jnp.float32),
            pltpu.VMEM((512, 2 * CHUNK), jnp.bfloat16),
            pltpu.VMEM((512, 2 * CHUNK), jnp.bfloat16),
            pltpu.VMEM((512, LAGS), jnp.float32),
            pltpu.VMEM((512, LAGS), jnp.float32),
            pltpu.VMEM((2 * BINS, LAGS), jnp.bfloat16),
            pltpu.SemaphoreType.DMA,
        ],
        compiler_params=pltpu.CompilerParams(vmem_limit_bytes=40 * 1024 * 1024),
    )(place, mine, other, own, table)


def finish_kernel(group_ref, mask_ref, parts_ref, out_ref):
    first = group_ref[0] * 8
    upper = lax.broadcasted_iota(jnp.int32, (8, 1), 0) < 4
    for pair in range(2):
        sums, masks = [], []
        for x in (2 * pair, 2 * pair + 1):
            total = None
            for y in range(4):
                part = parts_ref[(x * 4 + y) * 32 : (x * 4 + y) * 32 + 32, :].astype(jnp.float32)
                total = part if total is None else total + part
            sums.append(total)
            masks.append(
                jnp.where(
                    upper,
                    mask_ref[0, first + 2 * x].astype(jnp.float32),
                    mask_ref[0, first + 2 * x + 1].astype(jnp.float32),
                )
            )
        for i in range(4):
            rows = jnp.concatenate([s[8 * i : 8 * i + 8] * m for s, m in zip(sums, masks)], axis=0)
            out_ref[i, 16 * pair : 16 * pair + 16, :] = rows.astype(jnp.bfloat16)


def finish(group, block_mask, parts):
    return pl.pallas_call(
        finish_kernel,
        out_shape=jax.ShapeDtypeStruct((4, 32, LAGS), jnp.bfloat16),
        in_specs=[SMEM, SMEM, VMEM],
        out_specs=VMEM,
    )(group, block_mask, parts)


def shards(table, spectra, quality, block_mask):
    white = whiten(spectra, quality)
    column = lax.all_gather(white, ("zh", "zl"))
    other = lax.ppermute(column, "core", [(0, 1), (1, 0)])
    zl = lax.axis_index("zl")
    own = lax.dynamic_slice_in_dim(column.reshape(2, 8, 8, BINS), zl, 1, axis=1)
    plane = lax.all_gather(own.reshape(16, BINS), "x")
    place = jnp.stack([lax.axis_index("zh"), lax.axis_index("core")]).astype(jnp.int32)
    partial = pairs(
        place, column.reshape(128, BINS), other.reshape(128, BINS), plane.reshape(64, BINS), table
    )
    parts = lax.all_to_all(partial.reshape(16, 32, LAGS), ("x", "y"), 0, 0, tiled=True)
    group = lax.axis_index(WIN).astype(jnp.int32).reshape(1)
    return finish(group, block_mask, parts.reshape(512, LAGS))


def solution(mesh):
    names, sizes = zip(*GRID)
    fine = Mesh(mesh.devices.reshape(sizes), names)
    placed = (P(None, WIN, STA, None), P(WIN, STA), P(STA, None))
    table = lag_table()

    def run(spectra, quality, block_mask):
        body = functools.partial(shards, jnp.asarray(table))
        return jax.shard_map(
            body, mesh=fine, in_specs=placed, out_specs=P(STA, WIN, None), check_vma=False
        )(spectra, quality, block_mask)

    return run
```

```python
import functools
import math

import jax
import jax.numpy as jnp
import ml_dtypes
import numpy as np
from jax import lax
from jax.experimental import pallas as pl
from jax.experimental.pallas import tpu as pltpu
from jax.sharding import Mesh, PartitionSpec as P

LAGS = 256
BINS = 2048
CHUNK = 256
CHUNKS = BINS // CHUNK
GRID = (("zl", 8), ("x", 4), ("core", 2), ("y", 4), ("zh", 2))
STA = ("zl", "x", "core")
WIN = ("y", "zh")
VMEM = pl.BlockSpec(memory_space=pltpu.VMEM)
SMEM = pl.BlockSpec(memory_space=pltpu.SMEM)
SMALL = pltpu.CompilerParams(vmem_limit_bytes=4 * 1024 * 1024)


def lag_table():
    phase = np.arange(BINS)[:, None] * (np.arange(LAGS)[None, :] - LAGS // 2) % (2 * BINS)
    angles = phase.astype(np.float32) * np.float32(math.pi / BINS)
    scale = np.float32(1.0 / math.sqrt(BINS))
    both = np.stack([np.cos(angles), -np.sin(angles)]).astype(np.float32) * scale
    both = both.reshape(2, CHUNKS, CHUNK, LAGS).transpose(1, 0, 2, 3).reshape(2 * BINS, LAGS)
    return both.astype(ml_dtypes.bfloat16)


def whiten_kernel(quality_ref, spectra_ref, white_ref):
    re = spectra_ref[0, 0].astype(jnp.float32)
    im = spectra_ref[1, 0].astype(jnp.float32)
    power_mean = jnp.mean(re * re + im * im, axis=-1, keepdims=True)
    row = lax.broadcasted_iota(jnp.int32, (4, 1), 0)
    flags = jnp.zeros((4, 1), jnp.float32)
    for s in range(4):
        flags = jnp.where(row == s, quality_ref[0, s].astype(jnp.float32), flags)
    scale = lax.rsqrt(power_mean + 1e-06) * flags
    white_ref[...] = jnp.concatenate([re * scale, im * scale], axis=0).astype(jnp.bfloat16)


def whiten(spectra, quality):
    return pl.pallas_call(
        whiten_kernel,
        out_shape=jax.ShapeDtypeStruct((8, BINS), jnp.bfloat16),
        in_specs=[SMEM, VMEM],
        out_specs=VMEM,
    )(quality, spectra)


def choose_kernel(half_ref, column_ref, sent_ref, chosen_ref):
    second = half_ref[0] == 1
    for w in range(2):
        parts = []
        for k in range(4):
            both = column_ref[(w * 8 + 2 * k) * 8 : (w * 8 + 2 * k) * 8 + 16, :].astype(jnp.float32)
            parts.append(jnp.where(second, both[8:16], both[0:8]))
        for c in range(2):
            rows = jnp.concatenate([p[4 * c : 4 * c + 4] for p in parts], axis=0)
            chosen_ref[(w * 2 + c) * 16 : (w * 2 + c) * 16 + 16, :] = rows.astype(jnp.bfloat16)


def choose(half, column, sent):
    return pl.pallas_call(
        choose_kernel,
        out_shape=jax.ShapeDtypeStruct((64, BINS), jnp.bfloat16),
        in_specs=[SMEM, VMEM, pl.BlockSpec(memory_space=pl.ANY)],
        out_specs=VMEM,
        compiler_params=SMALL,
    )(half, column, sent)


def pair_kernel(
    core_ref, mine_ref, other_ref, own_ref, table_hbm, out_ref,
    far, own, cross_even, cross_odd, total, order, table, arrived,
):
    fetch = pltpu.make_async_copy(table_hbm, table, arrived)
    fetch.start()
    core = core_ref[0]
    far[core] = mine_ref[...].astype(jnp.float32)
    far[1 - core] = other_ref[...].astype(jnp.float32)
    own[...] = own_ref[...].astype(jnp.float32)
    total[...] = jnp.zeros_like(total)

    def products(c, cross):
        bins = pl.ds(pl.multiple_of(c * CHUNK, CHUNK), CHUNK)
        for side in range(2):
            b_re = [far[side, 32 * w : 32 * w + 16, bins] for w in range(2)]
            b_im = [far[side, 32 * w + 16 : 32 * w + 32, bins] for w in range(2)]
            for i in range(16):
                re, im = None, None
                for w in range(2):
                    at = (i // 4) * 16 + w * 8 + i % 4
                    a_re = own[at : at + 1, bins]
                    a_im = own[at + 4 : at + 5, bins]
                    re_w = a_re * b_re[w] + a_im * b_im[w]
                    im_w = a_im * b_re[w] - a_re * b_im[w]
                    re = re_w if re is None else re + re_w
                    im = im_w if im is None else im + im_w
                to = side * 256 + i * 16
                cross[to : to + 16, 0:CHUNK] = re.astype(jnp.bfloat16)
                cross[to : to + 16, CHUNK : 2 * CHUNK] = im.astype(jnp.bfloat16)

    def to_lags(c, cross):
        rows = pl.ds(pl.multiple_of(c * 2 * CHUNK, 2 * CHUNK), 2 * CHUNK)
        total[...] += jnp.dot(cross[...], table[rows, :], preferred_element_type=jnp.float32)

    products(0, cross_even)
    fetch.wait()

    @pl.loop(0, CHUNKS // 2 - 1)
    def _(c):
        products(2 * c + 1, cross_odd)
        to_lags(2 * c, cross_even)
        products(2 * c + 2, cross_even)
        to_lags(2 * c + 1, cross_odd)

    products(CHUNKS - 1, cross_odd)
    to_lags(CHUNKS - 2, cross_even)
    to_lags(CHUNKS - 1, cross_odd)

    for side in range(2):
        for i in range(16):
            rows = total[side * 256 + i * 16 : side * 256 + i * 16 + 16, :]
            for k in range(4):
                to = ((i // 4) * 4 + k) * 32 + (i % 4) * 8 + side * 4
                order[to : to + 4, :] = rows[4 * k : 4 * k + 4]
    out_ref[...] = order[...].astype(jnp.bfloat16)


def pairs(core, mine, other, own, table):
    return pl.pallas_call(
        pair_kernel,
        out_shape=jax.ShapeDtypeStruct((512, LAGS), jnp.bfloat16),
        in_specs=[SMEM, VMEM, VMEM, VMEM, pl.BlockSpec(memory_space=pl.ANY)],
        out_specs=VMEM,
        scratch_shapes=[
            pltpu.VMEM((2, 64, BINS), jnp.float32),
            pltpu.VMEM((64, BINS), jnp.float32),
            pltpu.VMEM((512, 2 * CHUNK), jnp.bfloat16),
            pltpu.VMEM((512, 2 * CHUNK), jnp.bfloat16),
            pltpu.VMEM((512, LAGS), jnp.float32),
            pltpu.VMEM((512, LAGS), jnp.float32),
            pltpu.VMEM((2 * BINS, LAGS), jnp.bfloat16),
            pltpu.SemaphoreType.DMA,
        ],
        compiler_params=pltpu.CompilerParams(vmem_limit_bytes=40 * 1024 * 1024),
    )(core, mine, other, own, table)


def finish_kernel(group_ref, mask_ref, parts_ref, out_ref):
    first = group_ref[0] * 8
    upper = lax.broadcasted_iota(jnp.int32, (8, 1), 0) < 4
    for pair in range(2):
        sums, masks = [], []
        for x in (2 * pair, 2 * pair + 1):
            total = None
            for y in range(4):
                part = parts_ref[(x * 4 + y) * 32 : (x * 4 + y) * 32 + 32, :].astype(jnp.float32)
                total = part if total is None else total + part
            sums.append(total)
            masks.append(
                jnp.where(
                    upper,
                    mask_ref[0, first + 2 * x].astype(jnp.float32),
                    mask_ref[0, first + 2 * x + 1].astype(jnp.float32),
                )
            )
        for i in range(4):
            rows = jnp.concatenate([s[8 * i : 8 * i + 8] * m for s, m in zip(sums, masks)], axis=0)
            out_ref[i, 16 * pair : 16 * pair + 16, :] = rows.astype(jnp.bfloat16)


def finish(group, block_mask, parts):
    return pl.pallas_call(
        finish_kernel,
        out_shape=jax.ShapeDtypeStruct((4, 32, LAGS), jnp.bfloat16),
        in_specs=[SMEM, SMEM, VMEM],
        out_specs=VMEM,
        compiler_params=SMALL,
    )(group, block_mask, parts)


def shards(table, spectra, quality, block_mask):
    white = whiten(spectra, quality)
    column = lax.all_gather(white, ("zh", "zl"))
    zl = lax.axis_index("zl")
    own = lax.dynamic_slice_in_dim(column.reshape(2, 8, 8, BINS), zl, 1, axis=1)
    copies = jnp.broadcast_to(own.reshape(1, 16, BINS), (4, 16, BINS))
    plane = lax.all_to_all(copies, "x", 0, 0, tiled=True)
    half = lax.axis_index("zh").astype(jnp.int32).reshape(1)
    core = lax.axis_index("core").astype(jnp.int32).reshape(1)
    mine = choose(half, column.reshape(128, BINS), copies)
    other = lax.ppermute(mine, "core", [(0, 1), (1, 0)])
    partial = pairs(core, mine, other, plane.reshape(64, BINS), table)
    parts = lax.all_to_all(partial.reshape(16, 32, LAGS), ("x", "y"), 0, 0, tiled=True)
    group = lax.axis_index(WIN).astype(jnp.int32).reshape(1)
    return finish(group, block_mask, parts.reshape(512, LAGS))


def solution(mesh):
    names, sizes = zip(*GRID)
    fine = Mesh(mesh.devices.reshape(sizes), names)
    placed = (P(None, WIN, STA, None), P(WIN, STA), P(STA, None))
    table = lag_table()

    def run(spectra, quality, block_mask):
        body = functools.partial(shards, jnp.asarray(table))
        return jax.shard_map(
            body, mesh=fine, in_specs=placed, out_specs=P(STA, WIN, None), check_vma=False
        )(spectra, quality, block_mask)

    return run
```

```python
import functools
import math

import jax
import jax.numpy as jnp
import ml_dtypes
import numpy as np
from jax import lax
from jax.experimental import pallas as pl
from jax.experimental.pallas import tpu as pltpu
from jax.sharding import Mesh, PartitionSpec as P

LAGS = 256
BINS = 2048
CHUNK = 256
CHUNKS = BINS // CHUNK
GRID = (("zl", 8), ("x", 4), ("core", 2), ("y", 4), ("zh", 2))
STA = ("zl", "x", "core")
WIN = ("y", "zh")
VMEM = pl.BlockSpec(memory_space=pltpu.VMEM)
SMEM = pl.BlockSpec(memory_space=pltpu.SMEM)
SMALL = pltpu.CompilerParams(vmem_limit_bytes=4 * 1024 * 1024)


def lag_table():
    phase = np.arange(BINS)[:, None] * (np.arange(LAGS)[None, :] - LAGS // 2) % (2 * BINS)
    angles = phase.astype(np.float32) * np.float32(math.pi / BINS)
    scale = np.float32(1.0 / math.sqrt(BINS))
    both = np.stack([np.cos(angles), -np.sin(angles)]).astype(np.float32) * scale
    both = both.reshape(2, CHUNKS, CHUNK, LAGS).transpose(1, 0, 2, 3).reshape(2 * BINS, LAGS)
    return both.astype(ml_dtypes.bfloat16)


def whiten_kernel(quality_ref, spectra_ref, white_ref):
    re = spectra_ref[0, 0].astype(jnp.float32)
    im = spectra_ref[1, 0].astype(jnp.float32)
    power_mean = jnp.mean(re * re + im * im, axis=-1, keepdims=True)
    row = lax.broadcasted_iota(jnp.int32, (4, 1), 0)
    flags = jnp.zeros((4, 1), jnp.float32)
    for s in range(4):
        flags = jnp.where(row == s, quality_ref[0, s].astype(jnp.float32), flags)
    scale = lax.rsqrt(power_mean + 1e-06) * flags
    white_ref[...] = jnp.concatenate([re * scale, im * scale], axis=0).astype(jnp.bfloat16)


def whiten(spectra, quality):
    return pl.pallas_call(
        whiten_kernel,
        out_shape=jax.ShapeDtypeStruct((8, BINS), jnp.bfloat16),
        in_specs=[SMEM, VMEM],
        out_specs=VMEM,
    )(quality, spectra)


def choose_kernel(half_ref, column_ref, sent_ref, chosen_ref):
    second = half_ref[0] == 1
    for w in range(2):
        parts = []
        for k in range(4):
            both = column_ref[(w * 8 + 2 * k) * 8 : (w * 8 + 2 * k) * 8 + 16, :].astype(jnp.float32)
            parts.append(jnp.where(second, both[8:16], both[0:8]))
        for c in range(2):
            rows = jnp.concatenate([p[4 * c : 4 * c + 4] for p in parts], axis=0)
            chosen_ref[(w * 2 + c) * 16 : (w * 2 + c) * 16 + 16, :] = rows.astype(jnp.bfloat16)


def choose(half, column, sent):
    return pl.pallas_call(
        choose_kernel,
        out_shape=jax.ShapeDtypeStruct((64, BINS), jnp.bfloat16),
        in_specs=[SMEM, VMEM, pl.BlockSpec(memory_space=pl.ANY)],
        out_specs=VMEM,
        compiler_params=SMALL,
    )(half, column, sent)


def correlate(stations, far, own, crosses, total, table, ready):
    total[...] = jnp.zeros_like(total)

    def products(c, cross):
        bins = pl.ds(pl.multiple_of(c * CHUNK, CHUNK), CHUNK)
        for side in range(2):
            b_re = [far[side, 32 * w : 32 * w + 16, bins] for w in range(2)]
            b_im = [far[side, 32 * w + 16 : 32 * w + 32, bins] for w in range(2)]
            for i in range(stations):
                re, im = None, None
                for w in range(2):
                    at = (i // 4) * 16 + w * 8 + i % 4
                    a_re = own[at : at + 1, bins]
                    a_im = own[at + 4 : at + 5, bins]
                    re_w = a_re * b_re[w] + a_im * b_im[w]
                    im_w = a_im * b_re[w] - a_re * b_im[w]
                    re = re_w if re is None else re + re_w
                    im = im_w if im is None else im + im_w
                to = (side * stations + i) * 16
                cross[to : to + 16, 0:CHUNK] = re.astype(jnp.bfloat16)
                cross[to : to + 16, CHUNK : 2 * CHUNK] = im.astype(jnp.bfloat16)

    def to_lags(c, cross):
        rows = pl.ds(pl.multiple_of(c * 2 * CHUNK, 2 * CHUNK), 2 * CHUNK)
        total[...] += jnp.dot(cross[...], table[rows, :], preferred_element_type=jnp.float32)

    even, odd = crosses
    products(0, even)
    ready()

    @pl.loop(0, CHUNKS // 2 - 1)
    def _(c):
        products(2 * c + 1, odd)
        to_lags(2 * c, even)
        products(2 * c + 2, even)
        to_lags(2 * c + 1, odd)

    products(CHUNKS - 1, odd)
    to_lags(CHUNKS - 2, even)
    to_lags(CHUNKS - 1, odd)


def reorder(stations, total, order):
    for side in range(2):
        for i in range(stations):
            first = (side * stations + i) * 16
            rows = total[first : first + 16, :]
            for k in range(4):
                to = ((i // 4) * 4 + k) * 32 + (i % 4) * 8 + side * 4
                order[to : to + 4, :] = rows[4 * k : 4 * k + 4]


def own_pairs_kernel(
    far_ref, own_ref, table_hbm, out_ref,
    far, own, even, odd, total, order, table, arrived,
):
    fetch = pltpu.make_async_copy(table_hbm, table, arrived)
    fetch.start()
    far[...] = far_ref[...].astype(jnp.float32)
    own[...] = own_ref[...].astype(jnp.float32)
    correlate(4, far, own, (even, odd), total, table, fetch.wait)
    reorder(4, total, order)
    out_ref[...] = order[...].astype(jnp.bfloat16)


def plane_pairs_kernel(
    x_ref, far_ref, plane_ref, own_part_ref, table_hbm, out_ref,
    far, own, even, odd, total, order, table, arrived,
):
    fetch = pltpu.make_async_copy(table_hbm, table, arrived)
    fetch.start()
    far[...] = far_ref[...].astype(jnp.float32)
    x = x_ref[0]
    for n in range(3):
        block = lax.rem(x + n + 1, 4)
        own[16 * n : 16 * n + 16, :] = plane_ref[pl.ds(pl.multiple_of(block * 16, 16), 16), :].astype(jnp.float32)
    out_ref[pl.ds(pl.multiple_of(x * 128, 128), 128), :] = own_part_ref[...]
    correlate(12, far, own, (even, odd), total, table, fetch.wait)
    reorder(12, total, order)
    for n in range(3):
        block = lax.rem(x + n + 1, 4)
        rows = order[128 * n : 128 * n + 128, :].astype(jnp.bfloat16)
        out_ref[pl.ds(pl.multiple_of(block * 128, 128), 128), :] = rows


def pairs(kernel, blocks, result_rows, *operands):
    rows = blocks * 128
    specs = [SMEM if o.dtype == jnp.int32 else VMEM for o in operands]
    specs[-1] = pl.BlockSpec(memory_space=pl.ANY)
    return pl.pallas_call(
        kernel,
        out_shape=jax.ShapeDtypeStruct((result_rows, LAGS), jnp.bfloat16),
        in_specs=specs,
        out_specs=VMEM,
        scratch_shapes=[
            pltpu.VMEM((2, 64, BINS), jnp.float32),
            pltpu.VMEM((16 * blocks, BINS), jnp.float32),
            pltpu.VMEM((rows, 2 * CHUNK), jnp.bfloat16),
            pltpu.VMEM((rows, 2 * CHUNK), jnp.bfloat16),
            pltpu.VMEM((rows, LAGS), jnp.float32),
            pltpu.VMEM((rows, LAGS), jnp.float32),
            pltpu.VMEM((2 * BINS, LAGS), jnp.bfloat16),
            pltpu.SemaphoreType.DMA,
        ],
        compiler_params=pltpu.CompilerParams(vmem_limit_bytes=40 * 1024 * 1024),
        cost_estimate=pl.CostEstimate(
            flops=4 * rows * BINS * LAGS, bytes_accessed=6 * 2**20, transcendentals=0
        ),
    )(*operands)


def finish_kernel(group_ref, mask_ref, parts_ref, out_ref):
    first = group_ref[0] * 8
    upper = lax.broadcasted_iota(jnp.int32, (8, 1), 0) < 4
    for pair in range(2):
        sums, masks = [], []
        for x in (2 * pair, 2 * pair + 1):
            total = None
            for y in range(4):
                part = parts_ref[(x * 4 + y) * 32 : (x * 4 + y) * 32 + 32, :].astype(jnp.float32)
                total = part if total is None else total + part
            sums.append(total)
            masks.append(
                jnp.where(
                    upper,
                    mask_ref[0, first + 2 * x].astype(jnp.float32),
                    mask_ref[0, first + 2 * x + 1].astype(jnp.float32),
                )
            )
        for i in range(4):
            rows = jnp.concatenate([s[8 * i : 8 * i + 8] * m for s, m in zip(sums, masks)], axis=0)
            out_ref[i, 16 * pair : 16 * pair + 16, :] = rows.astype(jnp.bfloat16)


def finish(group, block_mask, parts):
    return pl.pallas_call(
        finish_kernel,
        out_shape=jax.ShapeDtypeStruct((4, 32, LAGS), jnp.bfloat16),
        in_specs=[SMEM, SMEM, VMEM],
        out_specs=VMEM,
        compiler_params=SMALL,
    )(group, block_mask, parts)


def shards(table, spectra, quality, block_mask):
    white = whiten(spectra, quality)
    column = lax.all_gather(white, ("zh", "zl"))
    zl = lax.axis_index("zl")
    own = lax.dynamic_slice_in_dim(column.reshape(2, 8, 8, BINS), zl, 1, axis=1)
    copies = jnp.broadcast_to(own.reshape(1, 16, BINS), (4, 16, BINS))
    plane = lax.all_to_all(copies, "x", 0, 0, tiled=True)
    half = lax.axis_index("zh").astype(jnp.int32).reshape(1)
    mine = choose(half, column.reshape(128, BINS), copies)
    far = lax.all_gather(mine, "core")
    x = lax.axis_index("x").astype(jnp.int32).reshape(1)
    own_part = pairs(own_pairs_kernel, 1, 128, far, own.reshape(16, BINS), table)
    partial = pairs(
        plane_pairs_kernel, 3, 512, x, far, plane.reshape(64, BINS), own_part, table
    )
    parts = lax.all_to_all(partial.reshape(16, 32, LAGS), ("x", "y"), 0, 0, tiled=True)
    group = lax.axis_index(WIN).astype(jnp.int32).reshape(1)
    return finish(group, block_mask, parts.reshape(512, LAGS))


def solution(mesh):
    names, sizes = zip(*GRID)
    fine = Mesh(mesh.devices.reshape(sizes), names)
    placed = (P(None, WIN, STA, None), P(WIN, STA), P(STA, None))
    table = lag_table()

    def run(spectra, quality, block_mask):
        body = functools.partial(shards, jnp.asarray(table))
        return jax.shard_map(
            body, mesh=fine, in_specs=placed, out_specs=P(STA, WIN, None), check_vma=False
        )(spectra, quality, block_mask)

    return run
```

```python
import functools
import math

import jax
import jax.numpy as jnp
import ml_dtypes
import numpy as np
from jax import lax
from jax.experimental import pallas as pl
from jax.experimental.pallas import tpu as pltpu
from jax.sharding import Mesh, PartitionSpec as P

LAGS = 256
BINS = 2048
CHUNK = 256
CHUNKS = BINS // CHUNK
STEP = 2
STEPS = CHUNKS // STEP
GRID = (("zl", 8), ("x", 4), ("core", 2), ("y", 4), ("zh", 2))
STA = ("zl", "x", "core")
WIN = ("y", "zh")
VMEM = pl.BlockSpec(memory_space=pltpu.VMEM)
SMEM = pl.BlockSpec(memory_space=pltpu.SMEM)
SMALL = pltpu.CompilerParams(vmem_limit_bytes=4 * 1024 * 1024)


def lag_table():
    phase = np.arange(BINS)[:, None] * (np.arange(LAGS)[None, :] - LAGS // 2) % (2 * BINS)
    angles = phase.astype(np.float32) * np.float32(math.pi / BINS)
    scale = np.float32(1.0 / math.sqrt(BINS))
    both = np.stack([np.cos(angles), -np.sin(angles)]).astype(np.float32) * scale
    both = both.reshape(2, CHUNKS, CHUNK, LAGS).transpose(1, 0, 2, 3).reshape(2 * BINS, LAGS)
    return both.astype(ml_dtypes.bfloat16)


def whiten_kernel(quality_ref, spectra_ref, white_ref):
    re = spectra_ref[0, 0].astype(jnp.float32)
    im = spectra_ref[1, 0].astype(jnp.float32)
    power_mean = jnp.mean(re * re + im * im, axis=-1, keepdims=True)
    row = lax.broadcasted_iota(jnp.int32, (4, 1), 0)
    flags = jnp.zeros((4, 1), jnp.float32)
    for s in range(4):
        flags = jnp.where(row == s, quality_ref[0, s].astype(jnp.float32), flags)
    scale = lax.rsqrt(power_mean + 1e-06) * flags
    white_ref[...] = jnp.concatenate([re * scale, im * scale], axis=0).astype(jnp.bfloat16)


def whiten(spectra, quality):
    return pl.pallas_call(
        whiten_kernel,
        out_shape=jax.ShapeDtypeStruct((8, BINS), jnp.bfloat16),
        in_specs=[SMEM, VMEM],
        out_specs=VMEM,
    )(quality, spectra)


def choose_kernel(half_ref, column_ref, sent_ref, chosen_ref):
    second = half_ref[0] == 1
    for w in range(2):
        parts = []
        for k in range(4):
            both = column_ref[(w * 8 + 2 * k) * 8 : (w * 8 + 2 * k) * 8 + 16, :].astype(jnp.float32)
            parts.append(jnp.where(second, both[8:16], both[0:8]))
        for c in range(2):
            rows = jnp.concatenate([p[4 * c : 4 * c + 4] for p in parts], axis=0)
            chosen_ref[(w * 2 + c) * 16 : (w * 2 + c) * 16 + 16, :] = rows.astype(jnp.bfloat16)


def choose(half, column, sent):
    return pl.pallas_call(
        choose_kernel,
        out_shape=jax.ShapeDtypeStruct((64, BINS), jnp.bfloat16),
        in_specs=[SMEM, VMEM, pl.BlockSpec(memory_space=pl.ANY)],
        out_specs=VMEM,
        compiler_params=SMALL,
    )(half, column, sent)


def correlate(stations, far, own, crosses, total, table):
    total[...] = jnp.zeros_like(total)

    def products(step, cross):
        for part in range(STEP):
            bins = pl.ds(pl.multiple_of((step * STEP + part) * CHUNK, CHUNK), CHUNK)
            for side in range(2):
                b_re = [far[side, 32 * w : 32 * w + 16, bins] for w in range(2)]
                b_im = [far[side, 32 * w + 16 : 32 * w + 32, bins] for w in range(2)]
                for i in range(stations):
                    re, im = None, None
                    for w in range(2):
                        at = (i // 4) * 16 + w * 8 + i % 4
                        a_re = own[at : at + 1, bins]
                        a_im = own[at + 4 : at + 5, bins]
                        re_w = a_re * b_re[w] + a_im * b_im[w]
                        im_w = a_im * b_re[w] - a_re * b_im[w]
                        re = re_w if re is None else re + re_w
                        im = im_w if im is None else im + im_w
                    to, first = (side * stations + i) * 16, 2 * CHUNK * part
                    cross[to : to + 16, first : first + CHUNK] = re.astype(jnp.bfloat16)
                    cross[to : to + 16, first + CHUNK : first + 2 * CHUNK] = im.astype(jnp.bfloat16)

    def to_lags(step, cross):
        depth = 2 * CHUNK * STEP
        rows = pl.ds(pl.multiple_of(step * depth, depth), depth)
        total[...] += jnp.dot(cross[...], table[rows, :], preferred_element_type=jnp.float32)

    even, odd = crosses
    products(0, even)

    @pl.loop(0, STEPS // 2 - 1)
    def _(n):
        products(2 * n + 1, odd)
        to_lags(2 * n, even)
        products(2 * n + 2, even)
        to_lags(2 * n + 1, odd)

    products(STEPS - 1, odd)
    to_lags(STEPS - 2, even)
    to_lags(STEPS - 1, odd)


def reorder(stations, total, order):
    for side in range(2):
        for i in range(stations):
            first = (side * stations + i) * 16
            rows = total[first : first + 16, :]
            for k in range(4):
                to = ((i // 4) * 4 + k) * 32 + (i % 4) * 8 + side * 4
                order[to : to + 4, :] = rows[4 * k : 4 * k + 4]


def own_pairs_kernel(
    far_ref, own_ref, table, out_ref,
    far, own, even, odd, total, order,
):
    far[...] = far_ref[...].astype(jnp.float32)
    own[...] = own_ref[...].astype(jnp.float32)
    correlate(4, far, own, (even, odd), total, table)
    reorder(4, total, order)
    out_ref[...] = order[...].astype(jnp.bfloat16)


def plane_pairs_kernel(
    x_ref, far_ref, plane_ref, own_part_ref, table, out_ref,
    far, own, even, odd, total, order,
):
    far[...] = far_ref[...].astype(jnp.float32)
    x = x_ref[0]
    for n in range(3):
        block = lax.rem(x + n + 1, 4)
        own[16 * n : 16 * n + 16, :] = plane_ref[pl.ds(pl.multiple_of(block * 16, 16), 16), :].astype(jnp.float32)
    out_ref[pl.ds(pl.multiple_of(x * 128, 128), 128), :] = own_part_ref[...]
    correlate(12, far, own, (even, odd), total, table)
    reorder(12, total, order)
    for n in range(3):
        block = lax.rem(x + n + 1, 4)
        rows = order[128 * n : 128 * n + 128, :].astype(jnp.bfloat16)
        out_ref[pl.ds(pl.multiple_of(block * 128, 128), 128), :] = rows


def pairs(kernel, blocks, result_rows, *operands):
    rows = blocks * 128
    specs = [SMEM if o.dtype == jnp.int32 else VMEM for o in operands]
    return pl.pallas_call(
        kernel,
        out_shape=jax.ShapeDtypeStruct((result_rows, LAGS), jnp.bfloat16),
        in_specs=specs,
        out_specs=VMEM,
        scratch_shapes=[
            pltpu.VMEM((2, 64, BINS), jnp.float32),
            pltpu.VMEM((16 * blocks, BINS), jnp.float32),
            pltpu.VMEM((rows, 2 * CHUNK * STEP), jnp.bfloat16),
            pltpu.VMEM((rows, 2 * CHUNK * STEP), jnp.bfloat16),
            pltpu.VMEM((rows, LAGS), jnp.float32),
            pltpu.VMEM((rows, LAGS), jnp.float32),
        ],
        compiler_params=pltpu.CompilerParams(vmem_limit_bytes=40 * 1024 * 1024),
        cost_estimate=pl.CostEstimate(
            flops=4 * rows * BINS * LAGS, bytes_accessed=6 * 2**20, transcendentals=0
        ),
    )(*operands)


def finish_kernel(group_ref, mask_ref, parts_ref, out_ref):
    first = group_ref[0] * 8
    upper = lax.broadcasted_iota(jnp.int32, (8, 1), 0) < 4
    for pair in range(2):
        sums, masks = [], []
        for x in (2 * pair, 2 * pair + 1):
            total = None
            for y in range(4):
                part = parts_ref[(x * 4 + y) * 32 : (x * 4 + y) * 32 + 32, :].astype(jnp.float32)
                total = part if total is None else total + part
            sums.append(total)
            masks.append(
                jnp.where(
                    upper,
                    mask_ref[0, first + 2 * x].astype(jnp.float32),
                    mask_ref[0, first + 2 * x + 1].astype(jnp.float32),
                )
            )
        for i in range(4):
            rows = jnp.concatenate([s[8 * i : 8 * i + 8] * m for s, m in zip(sums, masks)], axis=0)
            out_ref[i, 16 * pair : 16 * pair + 16, :] = rows.astype(jnp.bfloat16)


def finish(group, block_mask, parts):
    return pl.pallas_call(
        finish_kernel,
        out_shape=jax.ShapeDtypeStruct((4, 32, LAGS), jnp.bfloat16),
        in_specs=[SMEM, SMEM, VMEM],
        out_specs=VMEM,
        compiler_params=SMALL,
    )(group, block_mask, parts)


def shards(table, spectra, quality, block_mask):
    white = whiten(spectra, quality)
    column = lax.all_gather(white, ("zh", "zl"))
    zl = lax.axis_index("zl")
    own = lax.dynamic_slice_in_dim(column.reshape(2, 8, 8, BINS), zl, 1, axis=1)
    copies = jnp.broadcast_to(own.reshape(1, 16, BINS), (4, 16, BINS))
    plane = lax.all_to_all(copies, "x", 0, 0, tiled=True)
    half = lax.axis_index("zh").astype(jnp.int32).reshape(1)
    mine = choose(half, column.reshape(128, BINS), copies)
    far = lax.all_gather(mine, "core")
    x = lax.axis_index("x").astype(jnp.int32).reshape(1)
    own_part = pairs(own_pairs_kernel, 1, 128, far, own.reshape(16, BINS), table)
    partial = pairs(
        plane_pairs_kernel, 3, 512, x, far, plane.reshape(64, BINS), own_part, table
    )
    parts = lax.all_to_all(partial.reshape(16, 32, LAGS), ("x", "y"), 0, 0, tiled=True)
    group = lax.axis_index(WIN).astype(jnp.int32).reshape(1)
    return finish(group, block_mask, parts.reshape(512, LAGS))


def solution(mesh):
    names, sizes = zip(*GRID)
    fine = Mesh(mesh.devices.reshape(sizes), names)
    placed = (P(None, WIN, STA, None), P(WIN, STA), P(STA, None))
    table = lag_table()

    def run(spectra, quality, block_mask):
        body = functools.partial(shards, jnp.asarray(table))
        return jax.shard_map(
            body, mesh=fine, in_specs=placed, out_specs=P(STA, WIN, None), check_vma=False
        )(spectra, quality, block_mask)

    return run
```

```python
import functools
import math

import jax
import jax.numpy as jnp
import ml_dtypes
import numpy as np
from jax import lax
from jax.experimental import pallas as pl
from jax.experimental.pallas import tpu as pltpu
from jax.sharding import Mesh, PartitionSpec as P

LAGS = 256
BINS = 2048
CHUNK = 256
CHUNKS = BINS // CHUNK
STEP = 2
STEPS = CHUNKS // STEP
GRID = (("zl", 8), ("x", 4), ("core", 2), ("y", 4), ("zh", 2))
STA = ("zl", "x", "core")
WIN = ("y", "zh")
VMEM = pl.BlockSpec(memory_space=pltpu.VMEM)
SMEM = pl.BlockSpec(memory_space=pltpu.SMEM)
SMALL = pltpu.CompilerParams(vmem_limit_bytes=4 * 1024 * 1024)


def lag_table():
    phase = np.arange(BINS)[:, None] * (np.arange(LAGS)[None, :] - LAGS // 2) % (2 * BINS)
    angles = phase.astype(np.float32) * np.float32(math.pi / BINS)
    scale = np.float32(1.0 / math.sqrt(BINS))
    both = np.stack([np.cos(angles), -np.sin(angles)]).astype(np.float32) * scale
    both = both.reshape(2, CHUNKS, CHUNK, LAGS).transpose(1, 0, 2, 3).reshape(2 * BINS, LAGS)
    return both.astype(ml_dtypes.bfloat16)


def whiten_kernel(quality_ref, spectra_ref, white_ref):
    re = spectra_ref[0, 0].astype(jnp.float32)
    im = spectra_ref[1, 0].astype(jnp.float32)
    power_mean = jnp.mean(re * re + im * im, axis=-1, keepdims=True)
    row = lax.broadcasted_iota(jnp.int32, (4, 1), 0)
    flags = jnp.zeros((4, 1), jnp.float32)
    for s in range(4):
        flags = jnp.where(row == s, quality_ref[0, s].astype(jnp.float32), flags)
    scale = lax.rsqrt(power_mean + 1e-06) * flags
    white_ref[...] = jnp.concatenate([re * scale, im * scale], axis=0).astype(jnp.bfloat16)


def whiten(spectra, quality):
    return pl.pallas_call(
        whiten_kernel,
        out_shape=jax.ShapeDtypeStruct((8, BINS), jnp.bfloat16),
        in_specs=[SMEM, VMEM],
        out_specs=VMEM,
    )(quality, spectra)


def choose_kernel(column_ref, sent_ref, chosen_ref):
    second = lax.axis_index("zh") == 1
    for w in range(2):
        parts = []
        for k in range(4):
            both = column_ref[(w * 8 + 2 * k) * 8 : (w * 8 + 2 * k) * 8 + 16, :].astype(jnp.float32)
            parts.append(jnp.where(second, both[8:16], both[0:8]))
        for c in range(2):
            rows = jnp.concatenate([p[4 * c : 4 * c + 4] for p in parts], axis=0)
            chosen_ref[(w * 2 + c) * 16 : (w * 2 + c) * 16 + 16, :] = rows.astype(jnp.bfloat16)


def choose(column, sent):
    return pl.pallas_call(
        choose_kernel,
        out_shape=jax.ShapeDtypeStruct((64, BINS), jnp.bfloat16),
        in_specs=[VMEM, pl.BlockSpec(memory_space=pl.ANY)],
        out_specs=VMEM,
        compiler_params=SMALL,
    )(column, sent)


def correlate(stations, far, own, crosses, total, table):
    total[...] = jnp.zeros_like(total)

    def products(step, cross):
        for part in range(STEP):
            bins = pl.ds(pl.multiple_of((step * STEP + part) * CHUNK, CHUNK), CHUNK)
            for side in range(2):
                b_re = [far[side, 32 * w : 32 * w + 16, bins] for w in range(2)]
                b_im = [far[side, 32 * w + 16 : 32 * w + 32, bins] for w in range(2)]
                for i in range(stations):
                    re, im = None, None
                    for w in range(2):
                        at = (i // 4) * 16 + w * 8 + i % 4
                        a_re = own[at : at + 1, bins]
                        a_im = own[at + 4 : at + 5, bins]
                        re_w = a_re * b_re[w] + a_im * b_im[w]
                        im_w = a_im * b_re[w] - a_re * b_im[w]
                        re = re_w if re is None else re + re_w
                        im = im_w if im is None else im + im_w
                    to, first = (side * stations + i) * 16, 2 * CHUNK * part
                    cross[to : to + 16, first : first + CHUNK] = re.astype(jnp.bfloat16)
                    cross[to : to + 16, first + CHUNK : first + 2 * CHUNK] = im.astype(jnp.bfloat16)

    def to_lags(step, cross):
        depth = 2 * CHUNK * STEP
        rows = pl.ds(pl.multiple_of(step * depth, depth), depth)
        total[...] += jnp.dot(cross[...], table[rows, :], preferred_element_type=jnp.float32)

    even, odd = crosses
    products(0, even)

    @pl.loop(0, STEPS // 2 - 1)
    def _(n):
        products(2 * n + 1, odd)
        to_lags(2 * n, even)
        products(2 * n + 2, even)
        to_lags(2 * n + 1, odd)

    products(STEPS - 1, odd)
    to_lags(STEPS - 2, even)
    to_lags(STEPS - 1, odd)


def reorder(stations, total, order):
    for side in range(2):
        for i in range(stations):
            first = (side * stations + i) * 16
            rows = total[first : first + 16, :]
            for k in range(4):
                to = ((i // 4) * 4 + k) * 32 + (i % 4) * 8 + side * 4
                order[to : to + 4, :] = rows[4 * k : 4 * k + 4]


def own_pairs_kernel(
    far_ref, own_ref, table, out_ref,
    far, own, even, odd, total, order,
):
    far[...] = far_ref[...].astype(jnp.float32)
    own[...] = own_ref[...].astype(jnp.float32)
    correlate(4, far, own, (even, odd), total, table)
    reorder(4, total, order)
    out_ref[...] = order[...].astype(jnp.bfloat16)


def plane_pairs_kernel(
    far_ref, plane_ref, own_part_ref, table, out_ref,
    far, own, even, odd, total, order,
):
    far[...] = far_ref[...].astype(jnp.float32)
    x = lax.axis_index("x")
    for n in range(3):
        block = lax.rem(x + n + 1, 4)
        own[16 * n : 16 * n + 16, :] = plane_ref[pl.ds(pl.multiple_of(block * 16, 16), 16), :].astype(jnp.float32)
    out_ref[pl.ds(pl.multiple_of(x * 128, 128), 128), :] = own_part_ref[...]
    correlate(12, far, own, (even, odd), total, table)
    reorder(12, total, order)
    for n in range(3):
        block = lax.rem(x + n + 1, 4)
        rows = order[128 * n : 128 * n + 128, :].astype(jnp.bfloat16)
        out_ref[pl.ds(pl.multiple_of(block * 128, 128), 128), :] = rows


def pairs(kernel, blocks, result_rows, *operands):
    rows = blocks * 128
    return pl.pallas_call(
        kernel,
        out_shape=jax.ShapeDtypeStruct((result_rows, LAGS), jnp.bfloat16),
        in_specs=[VMEM] * len(operands),
        out_specs=VMEM,
        scratch_shapes=[
            pltpu.VMEM((2, 64, BINS), jnp.float32),
            pltpu.VMEM((16 * blocks, BINS), jnp.float32),
            pltpu.VMEM((rows, 2 * CHUNK * STEP), jnp.bfloat16),
            pltpu.VMEM((rows, 2 * CHUNK * STEP), jnp.bfloat16),
            pltpu.VMEM((rows, LAGS), jnp.float32),
            pltpu.VMEM((rows, LAGS), jnp.float32),
        ],
        compiler_params=pltpu.CompilerParams(vmem_limit_bytes=40 * 1024 * 1024),
        cost_estimate=pl.CostEstimate(
            flops=4 * rows * BINS * LAGS, bytes_accessed=6 * 2**20, transcendentals=0
        ),
    )(*operands)


def finish_kernel(mask_ref, parts_ref, out_ref):
    first = (lax.axis_index("y") * 2 + lax.axis_index("zh")) * 8
    lane = lax.broadcasted_iota(jnp.int32, (8, 64), 1)
    core = lax.broadcasted_iota(jnp.int32, (8, 64), 0) // 4
    flags = jnp.broadcast_to(mask_ref[...].astype(jnp.float32), (8, 64))
    for pair in range(2):
        sums, masks = [], []
        for x in (2 * pair, 2 * pair + 1):
            total = None
            for y in range(4):
                part = parts_ref[(x * 4 + y) * 32 : (x * 4 + y) * 32 + 32, :].astype(jnp.float32)
                total = part if total is None else total + part
            sums.append(total)
            here = lane == first + 2 * x + core
            masks.append(jnp.sum(jnp.where(here, flags, 0.0), axis=1, keepdims=True))
        for i in range(4):
            rows = jnp.concatenate([s[8 * i : 8 * i + 8] * m for s, m in zip(sums, masks)], axis=0)
            out_ref[i, 16 * pair : 16 * pair + 16, :] = rows.astype(jnp.bfloat16)


def finish(block_mask, parts):
    return pl.pallas_call(
        finish_kernel,
        out_shape=jax.ShapeDtypeStruct((4, 32, LAGS), jnp.bfloat16),
        in_specs=[VMEM, VMEM],
        out_specs=VMEM,
        compiler_params=SMALL,
    )(block_mask, parts)


def shards(table, spectra, quality, block_mask):
    white = whiten(spectra, quality)
    column = lax.all_gather(white, ("zh", "zl"))
    zl = lax.axis_index("zl")
    own = lax.dynamic_slice_in_dim(column.reshape(2, 8, 8, BINS), zl, 1, axis=1)
    copies = jnp.broadcast_to(own.reshape(1, 16, BINS), (4, 16, BINS))
    plane = lax.all_to_all(copies, "x", 0, 0, tiled=True)
    mine = choose(column.reshape(128, BINS), copies)
    far = lax.all_gather(mine, "core")
    own_part = pairs(own_pairs_kernel, 1, 128, far, own.reshape(16, BINS), table)
    partial = pairs(
        plane_pairs_kernel, 3, 512, far, plane.reshape(64, BINS), own_part, table
    )
    parts = lax.all_to_all(partial.reshape(16, 32, LAGS), ("x", "y"), 0, 0, tiled=True)
    return finish(block_mask, parts.reshape(512, LAGS))


def solution(mesh):
    names, sizes = zip(*GRID)
    fine = Mesh(mesh.devices.reshape(sizes), names)
    placed = (P(None, WIN, STA, None), P(WIN, STA), P(STA, None))
    table = lag_table()

    def run(spectra, quality, block_mask):
        body = functools.partial(shards, jnp.asarray(table))
        return jax.shard_map(
            body, mesh=fine, in_specs=placed, out_specs=P(STA, WIN, None), check_vma=False
        )(spectra, quality, block_mask)

    return run
```

```python
import functools
import math

import jax
import jax.numpy as jnp
import ml_dtypes
import numpy as np
from jax import lax
from jax.experimental import pallas as pl
from jax.experimental.pallas import tpu as pltpu
from jax.sharding import Mesh, PartitionSpec as P

LAGS = 256
BINS = 2048
CHUNK = 256
CHUNKS = BINS // CHUNK
STEP = 2
STEPS = CHUNKS // STEP
GRID = (("zl", 8), ("x", 4), ("core", 2), ("y", 4), ("zh", 2))
STA = ("zl", "x", "core")
WIN = ("y", "zh")
VMEM = pl.BlockSpec(memory_space=pltpu.VMEM)
SMEM = pl.BlockSpec(memory_space=pltpu.SMEM)
SMALL = pltpu.CompilerParams(vmem_limit_bytes=4 * 1024 * 1024)


def lag_table():
    phase = np.arange(BINS)[:, None] * (np.arange(LAGS)[None, :] - LAGS // 2) % (2 * BINS)
    angles = phase.astype(np.float32) * np.float32(math.pi / BINS)
    scale = np.float32(1.0 / math.sqrt(BINS))
    both = np.stack([np.cos(angles), -np.sin(angles)]).astype(np.float32) * scale
    both = both.reshape(2, CHUNKS, CHUNK, LAGS).transpose(1, 0, 2, 3).reshape(2 * BINS, LAGS)
    return both.astype(ml_dtypes.bfloat16)


def whiten_kernel(quality_ref, values_ref, white_ref):
    re, im = values_ref[0, 0], values_ref[1, 0]
    power_mean = jnp.mean(re * re + im * im, axis=-1, keepdims=True)
    row = lax.broadcasted_iota(jnp.int32, (4, 4), 0)
    column = lax.broadcasted_iota(jnp.int32, (4, 4), 1)
    quality = jnp.broadcast_to(quality_ref[...].astype(jnp.float32), (4, 4))
    flags = jnp.sum(jnp.where(row == column, quality, 0.0), axis=1, keepdims=True)
    scale = lax.rsqrt(power_mean + 1e-06) * flags
    white_ref[...] = jnp.concatenate([re * scale, im * scale], axis=0).astype(jnp.bfloat16)


def whiten(spectra, quality):
    return pl.pallas_call(
        whiten_kernel,
        out_shape=jax.ShapeDtypeStruct((8, BINS), jnp.bfloat16),
        in_specs=[VMEM, VMEM],
        out_specs=VMEM,
        compiler_params=SMALL,
    )(quality, spectra.astype(jnp.float32))


def choose_kernel(column_ref, sent_ref, chosen_ref):
    second = lax.axis_index("zh") == 1
    for w in range(2):
        parts = []
        for k in range(4):
            both = column_ref[(w * 8 + 2 * k) * 8 : (w * 8 + 2 * k) * 8 + 16, :].astype(jnp.float32)
            parts.append(jnp.where(second, both[8:16], both[0:8]))
        for c in range(2):
            rows = jnp.concatenate([p[4 * c : 4 * c + 4] for p in parts], axis=0)
            chosen_ref[(w * 2 + c) * 16 : (w * 2 + c) * 16 + 16, :] = rows.astype(jnp.bfloat16)


def choose(column, sent):
    return pl.pallas_call(
        choose_kernel,
        out_shape=jax.ShapeDtypeStruct((64, BINS), jnp.bfloat16),
        in_specs=[VMEM, pl.BlockSpec(memory_space=pl.ANY)],
        out_specs=VMEM,
        compiler_params=SMALL,
    )(column, sent)


def correlate(stations, far, own, crosses, total, table):
    total[...] = jnp.zeros_like(total)

    def products(step, cross):
        for part in range(STEP):
            bins = pl.ds(pl.multiple_of((step * STEP + part) * CHUNK, CHUNK), CHUNK)
            for side in range(2):
                b_re = [far[side, 32 * w : 32 * w + 16, bins] for w in range(2)]
                b_im = [far[side, 32 * w + 16 : 32 * w + 32, bins] for w in range(2)]
                for i in range(stations):
                    re, im = None, None
                    for w in range(2):
                        at = (i // 4) * 16 + w * 8 + i % 4
                        a_re = own[at : at + 1, bins]
                        a_im = own[at + 4 : at + 5, bins]
                        re_w = a_re * b_re[w] + a_im * b_im[w]
                        im_w = a_im * b_re[w] - a_re * b_im[w]
                        re = re_w if re is None else re + re_w
                        im = im_w if im is None else im + im_w
                    to, first = (side * stations + i) * 16, 2 * CHUNK * part
                    cross[to : to + 16, first : first + CHUNK] = re.astype(jnp.bfloat16)
                    cross[to : to + 16, first + CHUNK : first + 2 * CHUNK] = im.astype(jnp.bfloat16)

    def to_lags(step, cross):
        depth = 2 * CHUNK * STEP
        rows = pl.ds(pl.multiple_of(step * depth, depth), depth)
        total[...] += jnp.dot(cross[...], table[rows, :], preferred_element_type=jnp.float32)

    even, odd = crosses
    products(0, even)

    @pl.loop(0, STEPS // 2 - 1)
    def _(n):
        products(2 * n + 1, odd)
        to_lags(2 * n, even)
        products(2 * n + 2, even)
        to_lags(2 * n + 1, odd)

    products(STEPS - 1, odd)
    to_lags(STEPS - 2, even)
    to_lags(STEPS - 1, odd)


def reorder(stations, total, order):
    for side in range(2):
        for i in range(stations):
            first = (side * stations + i) * 16
            rows = total[first : first + 16, :]
            for k in range(4):
                to = ((i // 4) * 4 + k) * 32 + (i % 4) * 8 + side * 4
                order[to : to + 4, :] = rows[4 * k : 4 * k + 4]


def own_pairs_kernel(
    far_ref, own_ref, table, out_ref,
    far, own, even, odd, total, order,
):
    far[...] = far_ref[...].astype(jnp.float32)
    own[...] = own_ref[...].astype(jnp.float32)
    correlate(4, far, own, (even, odd), total, table)
    reorder(4, total, order)
    out_ref[...] = order[...].astype(jnp.bfloat16)


def plane_pairs_kernel(
    far_ref, plane_ref, own_part_ref, table, out_ref,
    far, own, even, odd, total, order,
):
    far[...] = far_ref[...].astype(jnp.float32)
    x = lax.axis_index("x")
    for n in range(3):
        block = lax.rem(x + n + 1, 4)
        own[16 * n : 16 * n + 16, :] = plane_ref[pl.ds(pl.multiple_of(block * 16, 16), 16), :].astype(jnp.float32)
    out_ref[pl.ds(pl.multiple_of(x * 128, 128), 128), :] = own_part_ref[...]
    correlate(12, far, own, (even, odd), total, table)
    reorder(12, total, order)
    for n in range(3):
        block = lax.rem(x + n + 1, 4)
        rows = order[128 * n : 128 * n + 128, :].astype(jnp.bfloat16)
        out_ref[pl.ds(pl.multiple_of(block * 128, 128), 128), :] = rows


def pairs(kernel, blocks, result_rows, *operands):
    rows = blocks * 128
    return pl.pallas_call(
        kernel,
        out_shape=jax.ShapeDtypeStruct((result_rows, LAGS), jnp.bfloat16),
        in_specs=[VMEM] * len(operands),
        out_specs=VMEM,
        scratch_shapes=[
            pltpu.VMEM((2, 64, BINS), jnp.float32),
            pltpu.VMEM((16 * blocks, BINS), jnp.float32),
            pltpu.VMEM((rows, 2 * CHUNK * STEP), jnp.bfloat16),
            pltpu.VMEM((rows, 2 * CHUNK * STEP), jnp.bfloat16),
            pltpu.VMEM((rows, LAGS), jnp.float32),
            pltpu.VMEM((rows, LAGS), jnp.float32),
        ],
        compiler_params=pltpu.CompilerParams(vmem_limit_bytes=40 * 1024 * 1024),
        cost_estimate=pl.CostEstimate(
            flops=4 * rows * BINS * LAGS, bytes_accessed=6 * 2**20, transcendentals=0
        ),
    )(*operands)


def finish_kernel(mask_ref, parts_ref, out_ref):
    first = (lax.axis_index("y") * 2 + lax.axis_index("zh")) * 8
    lane = lax.broadcasted_iota(jnp.int32, (8, 64), 1)
    core = lax.broadcasted_iota(jnp.int32, (8, 64), 0) // 4
    flags = jnp.broadcast_to(mask_ref[...].astype(jnp.float32), (8, 64))
    for pair in range(2):
        sums, masks = [], []
        for x in (2 * pair, 2 * pair + 1):
            total = None
            for y in range(4):
                part = parts_ref[(x * 4 + y) * 32 : (x * 4 + y) * 32 + 32, :].astype(jnp.float32)
                total = part if total is None else total + part
            sums.append(total)
            here = lane == first + 2 * x + core
            masks.append(jnp.sum(jnp.where(here, flags, 0.0), axis=1, keepdims=True))
        for i in range(4):
            rows = jnp.concatenate([s[8 * i : 8 * i + 8] * m for s, m in zip(sums, masks)], axis=0)
            out_ref[i, 16 * pair : 16 * pair + 16, :] = rows.astype(jnp.bfloat16)


def finish(block_mask, parts):
    return pl.pallas_call(
        finish_kernel,
        out_shape=jax.ShapeDtypeStruct((4, 32, LAGS), jnp.bfloat16),
        in_specs=[VMEM, VMEM],
        out_specs=VMEM,
        compiler_params=SMALL,
    )(block_mask, parts)


def shards(table, spectra, quality, block_mask):
    white = whiten(spectra, quality)
    column = lax.all_gather(white, ("zh", "zl"))
    zl = lax.axis_index("zl")
    own = lax.dynamic_slice_in_dim(column.reshape(2, 8, 8, BINS), zl, 1, axis=1)
    copies = jnp.broadcast_to(own.reshape(1, 16, BINS), (4, 16, BINS))
    plane = lax.all_to_all(copies, "x", 0, 0, tiled=True)
    mine = choose(column.reshape(128, BINS), copies)
    far = lax.all_gather(mine, "core")
    own_part = pairs(own_pairs_kernel, 1, 128, far, own.reshape(16, BINS), table)
    partial = pairs(
        plane_pairs_kernel, 3, 512, far, plane.reshape(64, BINS), own_part, table
    )
    parts = lax.all_to_all(partial.reshape(16, 32, LAGS), ("x", "y"), 0, 0, tiled=True)
    return finish(block_mask, parts.reshape(512, LAGS))


def solution(mesh):
    names, sizes = zip(*GRID)
    fine = Mesh(mesh.devices.reshape(sizes), names)
    placed = (P(None, WIN, STA, None), P(WIN, STA), P(STA, None))
    table = lag_table()

    def run(spectra, quality, block_mask):
        body = functools.partial(shards, jnp.asarray(table))
        return jax.shard_map(
            body, mesh=fine, in_specs=placed, out_specs=P(STA, WIN, None), check_vma=False
        )(spectra, quality, block_mask)

    return run
```

```python
import functools
import math

import jax
import jax.numpy as jnp
import ml_dtypes
import numpy as np
from jax import lax
from jax.experimental import pallas as pl
from jax.experimental.pallas import tpu as pltpu
from jax.sharding import Mesh, PartitionSpec as P

LAGS = 256
BINS = 2048
CHUNK = 256
CHUNKS = BINS // CHUNK
STEP = 2
STEPS = CHUNKS // STEP
GRID = (("zl", 8), ("x", 4), ("core", 2), ("y", 4), ("zh", 2))
STA = ("zl", "x", "core")
WIN = ("y", "zh")
VMEM = pl.BlockSpec(memory_space=pltpu.VMEM)
SMEM = pl.BlockSpec(memory_space=pltpu.SMEM)
SMALL = pltpu.CompilerParams(vmem_limit_bytes=4 * 1024 * 1024)


def lag_table():
    phase = np.arange(BINS)[:, None] * (np.arange(LAGS)[None, :] - LAGS // 2) % (2 * BINS)
    angles = phase.astype(np.float32) * np.float32(math.pi / BINS)
    scale = np.float32(1.0 / math.sqrt(BINS))
    both = np.stack([np.cos(angles), -np.sin(angles)]).astype(np.float32) * scale
    both = both.reshape(2, CHUNKS, CHUNK, LAGS).transpose(1, 0, 2, 3).reshape(2 * BINS, LAGS)
    return both.astype(ml_dtypes.bfloat16)


def whiten_kernel(quality_ref, spectra_ref, white_ref):
    re = spectra_ref[0, 0].astype(jnp.float32)
    im = spectra_ref[1, 0].astype(jnp.float32)
    power_mean = jnp.mean(re * re + im * im, axis=-1, keepdims=True)
    row = lax.broadcasted_iota(jnp.int32, (4, 4), 0)
    column = lax.broadcasted_iota(jnp.int32, (4, 4), 1)
    quality = jnp.broadcast_to(quality_ref[...].astype(jnp.float32), (4, 4))
    flags = jnp.sum(jnp.where(row == column, quality, 0.0), axis=1, keepdims=True)
    scale = lax.rsqrt(power_mean + 1e-06) * flags
    white_ref[...] = jnp.concatenate([re * scale, im * scale], axis=0).astype(jnp.bfloat16)


def whiten(spectra, quality):
    return pl.pallas_call(
        whiten_kernel,
        out_shape=jax.ShapeDtypeStruct((8, BINS), jnp.bfloat16),
        in_specs=[VMEM, VMEM],
        out_specs=VMEM,
    )(quality, spectra)


def choose_kernel(column_ref, sent_ref, chosen_ref):
    second = lax.axis_index("zh") == 1
    for w in range(2):
        parts = []
        for k in range(4):
            both = column_ref[(w * 8 + 2 * k) * 8 : (w * 8 + 2 * k) * 8 + 16, :].astype(jnp.float32)
            parts.append(jnp.where(second, both[8:16], both[0:8]))
        for c in range(2):
            rows = jnp.concatenate([p[4 * c : 4 * c + 4] for p in parts], axis=0)
            chosen_ref[(w * 2 + c) * 16 : (w * 2 + c) * 16 + 16, :] = rows.astype(jnp.bfloat16)


def choose(column, sent):
    return pl.pallas_call(
        choose_kernel,
        out_shape=jax.ShapeDtypeStruct((64, BINS), jnp.bfloat16),
        in_specs=[VMEM, pl.BlockSpec(memory_space=pl.ANY)],
        out_specs=VMEM,
        compiler_params=SMALL,
    )(column, sent)


def correlate(stations, far, own, crosses, total, table):
    def products(step, cross):
        for part in range(STEP):
            bins = pl.ds(pl.multiple_of((step * STEP + part) * CHUNK, CHUNK), CHUNK)
            for side in range(2):
                b_re = [far[side, 32 * w : 32 * w + 16, bins] for w in range(2)]
                b_im = [far[side, 32 * w + 16 : 32 * w + 32, bins] for w in range(2)]
                for i in range(stations):
                    re, im = None, None
                    for w in range(2):
                        at = (i // 4) * 16 + w * 8 + i % 4
                        a_re = own[at : at + 1, bins]
                        a_im = own[at + 4 : at + 5, bins]
                        re_w = a_re * b_re[w] + a_im * b_im[w]
                        im_w = a_im * b_re[w] - a_re * b_im[w]
                        re = re_w if re is None else re + re_w
                        im = im_w if im is None else im + im_w
                    to, first = (side * stations + i) * 16, 2 * CHUNK * part
                    cross[to : to + 16, first : first + CHUNK] = re.astype(jnp.bfloat16)
                    cross[to : to + 16, first + CHUNK : first + 2 * CHUNK] = im.astype(jnp.bfloat16)

    def lags(step, cross):
        depth = 2 * CHUNK * STEP
        rows = pl.ds(pl.multiple_of(step * depth, depth), depth)
        return jnp.dot(cross[...], table[rows, :], preferred_element_type=jnp.float32)

    def to_lags(step, cross):
        total[...] += lags(step, cross)

    even, odd = crosses
    products(0, even)

    products(1, odd)
    total[...] = lags(0, even)
    for n in range(2, STEPS):
        products(n, crosses[n % 2])
        to_lags(n - 1, crosses[(n - 1) % 2])
    to_lags(STEPS - 1, crosses[(STEPS - 1) % 2])


def reorder(stations, total, order):
    for side in range(2):
        for i in range(stations):
            first = (side * stations + i) * 16
            rows = total[first : first + 16, :]
            for k in range(4):
                to = ((i // 4) * 4 + k) * 32 + (i % 4) * 8 + side * 4
                order[to : to + 4, :] = rows[4 * k : 4 * k + 4]


def own_pairs_kernel(
    far_ref, own_ref, table, out_ref,
    far, own, even, odd, total, order,
):
    far[...] = far_ref[...].astype(jnp.float32)
    own[...] = own_ref[...].astype(jnp.float32)
    correlate(4, far, own, (even, odd), total, table)
    reorder(4, total, order)
    out_ref[...] = order[...].astype(jnp.bfloat16)


def plane_pairs_kernel(
    far_ref, plane_ref, own_part_ref, table, out_ref,
    far, own, even, odd, total, order,
):
    far[...] = far_ref[...].astype(jnp.float32)
    x = lax.axis_index("x")
    for n in range(3):
        block = lax.rem(x + n + 1, 4)
        own[16 * n : 16 * n + 16, :] = plane_ref[pl.ds(pl.multiple_of(block * 16, 16), 16), :].astype(jnp.float32)
    out_ref[pl.ds(pl.multiple_of(x * 128, 128), 128), :] = own_part_ref[...]
    correlate(12, far, own, (even, odd), total, table)
    reorder(12, total, order)
    for n in range(3):
        block = lax.rem(x + n + 1, 4)
        rows = order[128 * n : 128 * n + 128, :].astype(jnp.bfloat16)
        out_ref[pl.ds(pl.multiple_of(block * 128, 128), 128), :] = rows


def pairs(kernel, blocks, result_rows, *operands):
    rows = blocks * 128
    return pl.pallas_call(
        kernel,
        out_shape=jax.ShapeDtypeStruct((result_rows, LAGS), jnp.bfloat16),
        in_specs=[VMEM] * len(operands),
        out_specs=VMEM,
        scratch_shapes=[
            pltpu.VMEM((2, 64, BINS), jnp.float32),
            pltpu.VMEM((16 * blocks, BINS), jnp.float32),
            pltpu.VMEM((rows, 2 * CHUNK * STEP), jnp.bfloat16),
            pltpu.VMEM((rows, 2 * CHUNK * STEP), jnp.bfloat16),
            pltpu.VMEM((rows, LAGS), jnp.float32),
            pltpu.VMEM((rows, LAGS), jnp.float32),
        ],
        compiler_params=pltpu.CompilerParams(vmem_limit_bytes=40 * 1024 * 1024),
        cost_estimate=pl.CostEstimate(
            flops=4 * rows * BINS * LAGS, bytes_accessed=6 * 2**20, transcendentals=0
        ),
    )(*operands)


def finish_kernel(mask_ref, parts_ref, out_ref):
    first = (lax.axis_index("y") * 2 + lax.axis_index("zh")) * 8
    lane = lax.broadcasted_iota(jnp.int32, (8, 64), 1)
    core = lax.broadcasted_iota(jnp.int32, (8, 64), 0) // 4
    flags = jnp.broadcast_to(mask_ref[...].astype(jnp.float32), (8, 64))
    for pair in range(2):
        sums, masks = [], []
        for x in (2 * pair, 2 * pair + 1):
            total = None
            for y in range(4):
                part = parts_ref[(x * 4 + y) * 32 : (x * 4 + y) * 32 + 32, :].astype(jnp.float32)
                total = part if total is None else total + part
            sums.append(total)
            here = lane == first + 2 * x + core
            masks.append(jnp.sum(jnp.where(here, flags, 0.0), axis=1, keepdims=True))
        for i in range(4):
            rows = jnp.concatenate([s[8 * i : 8 * i + 8] * m for s, m in zip(sums, masks)], axis=0)
            out_ref[i, 16 * pair : 16 * pair + 16, :] = rows.astype(jnp.bfloat16)


def finish(block_mask, parts):
    return pl.pallas_call(
        finish_kernel,
        out_shape=jax.ShapeDtypeStruct((4, 32, LAGS), jnp.bfloat16),
        in_specs=[VMEM, VMEM],
        out_specs=VMEM,
        compiler_params=SMALL,
    )(block_mask, parts)


def shards(table, spectra, quality, block_mask):
    white = whiten(spectra, quality)
    column = lax.all_gather(white, ("zh", "zl"))
    zl = lax.axis_index("zl")
    own = lax.dynamic_slice_in_dim(column.reshape(2, 8, 8, BINS), zl, 1, axis=1)
    copies = jnp.broadcast_to(own.reshape(1, 16, BINS), (4, 16, BINS))
    plane = lax.all_to_all(copies, "x", 0, 0, tiled=True)
    mine = choose(column.reshape(128, BINS), copies)
    far = lax.all_gather(mine, "core")
    own_part = pairs(own_pairs_kernel, 1, 128, far, own.reshape(16, BINS), table)
    partial = pairs(
        plane_pairs_kernel, 3, 512, far, plane.reshape(64, BINS), own_part, table
    )
    parts = lax.all_to_all(partial.reshape(16, 32, LAGS), ("x", "y"), 0, 0, tiled=True)
    return finish(block_mask, parts.reshape(512, LAGS))


def solution(mesh):
    names, sizes = zip(*GRID)
    fine = Mesh(mesh.devices.reshape(sizes), names)
    placed = (P(None, WIN, STA, None), P(WIN, STA), P(STA, None))
    table = lag_table()

    def run(spectra, quality, block_mask):
        body = functools.partial(shards, jnp.asarray(table))
        return jax.shard_map(
            body, mesh=fine, in_specs=placed, out_specs=P(STA, WIN, None), check_vma=False
        )(spectra, quality, block_mask)

    return run
```
